32 devices in a mesh: task: 4 (over y, x), width: 8 (over z, core).
Axes of the slice: x: 2, y: 2, z: 4, core: 2. Of those that a mesh axis runs over, the one named last changes fastest.
Arguments:
- task_ids: int32 [512], P('task'), may hold values from 0 to 1023
- embed_table: bfloat16 [1024, 1024], replicated, may hold values from -6 to 6
- trunk_weight: bfloat16 [1024, 2048], replicated, may hold values from -0.1875 to 0.1875
- trunk_bias: float32 [2048], replicated, may hold values from -6 to 6
- head_weight: bfloat16 [2048, 262144], P(None, ('task', 'width')), may hold values from -0.125 to 0.125
- head_bias: float32 [262144], P(('task', 'width')), may hold values from -4 to 4
- token_row: int32 [16384], P('task'), may hold values from 0 to 511, as said below
- inputs: bfloat16 [16384, 8192], P('task', 'width'), may hold values from -6 to 6
- frozen: bfloat16 [16384, 8192], P('task', 'width'), may hold values from -6 to 6
Outputs:
- adapted: bfloat16 [16384, 8192], P('task', 'width')
The draws below stay inside these ranges and needn't reach their ends.
Inputs may be any that keep to these rules, and one draw needn't show every extreme that they name: `token_row`: each of the 512 rows is named by exactly 32 tokens, and tokens b * 4096 to (b + 1) * 4096 - 1 name only rows b * 128 to (b + 1) * 128 - 1.
All inputs are finite; a program needn't handle non-finite values.
Results may differ from the reference program's by a relative error of at most 0.0061.
Values may be sent and summed in bfloat16 or wider, within the bound.
A program may use at most 192 MiB of HBM per device.

```python
import math
import jax
import jax.numpy as jnp
from jax import lax

TABLE = 1024
EMB = 1024
HID = 2048
WIDTH = 8192
RANK = 16
TOK_ROW = 32
ROWS_DEV = 128
ROWS = 512
TOK_DEV = 4096
TOKENS = 16384
COLS = 262144
N_WIDTH = 8


def draw_token_row(key, part):
    block_count = ROWS // ROWS_DEV
    key_list = jax.random.split(key, block_count)
    shuffled = jax.vmap(lambda subkey: jax.random.permutation(subkey, TOK_DEV))(key_list)
    local_rows = (shuffled % ROWS_DEV).astype(jnp.int32)
    offsets = jnp.arange(block_count, dtype=jnp.int32)[:, None] * ROWS_DEV
    return (local_rows + offsets).reshape(-1).astype(jnp.int32)


def with_ends(entries, own_key, least, top_value):
    spot = [jax.random.randint(jax.random.fold_in(own_key, axis), (), 0, length) for axis, length in enumerate(entries.shape)]
    widest = entries.shape.index(max(entries.shape))
    next_to = spot[:widest] + [(spot[widest] + 1) % entries.shape[widest]] + spot[widest + 1:]
    return entries.at[tuple(spot)].set(least).at[tuple(next_to)].set(top_value)


def block_levels(stream_key, shape, cuts, least, high):
    def one(axis_at, shards_of):
        steps = jax.random.uniform(jax.random.fold_in(jax.random.fold_in(stream_key, 6), axis_at), (shards_of,), jnp.float32, least / len(cuts), high / len(cuts))
        return jnp.repeat(jnp.exp(steps), shape[axis_at] // shards_of).reshape((-1,) + (1,) * (len(shape) - axis_at - 1))

    gain = one(*cuts[0])
    for cut in cuts[1:]:
        gain = gain * one(*cut)
    return gain


def bell_draw(own_key, extent, width, most, pieces=(), kind=jnp.bfloat16):
    gain = block_levels(own_key, extent, pieces, -0.22, 0.18) if pieces else 1.0
    array = jax.random.normal(own_key, extent, jnp.float32) * width * gain
    return jnp.minimum(jnp.maximum(array, -most), most).astype(kind)


def setup_inputs(seed: int = 0) -> dict:
    streams_of = jax.random.split(jax.random.key(seed), 10)
    return {
        "task_ids": with_ends(jax.random.randint(streams_of[0], (ROWS,), 0, TABLE), jax.random.fold_in(streams_of[0], 1), 0, TABLE - 1).astype(jnp.int32),
        "embed_table": bell_draw(streams_of[1], (TABLE, EMB), 1.0, 6.0),
        "trunk_weight": bell_draw(streams_of[2], (EMB, HID), EMB ** -0.5, 0.1875),
        "trunk_bias": bell_draw(streams_of[3], (HID,), 1.0, 6.0, (), jnp.float32),
        "head_weight": bell_draw(streams_of[4], (HID, COLS), HID ** -0.5, 0.125, ((1, 32),)),
        "head_bias": bell_draw(streams_of[5], (COLS,), 0.5, 4.0, ((0, 32),), jnp.float32),
        "token_row": draw_token_row(jax.random.fold_in(streams_of[9], 71), 0),
        "inputs": bell_draw(streams_of[7], (TOKENS, WIDTH), 1.0, 6.0, ((0, 4), (1, 8))),
        "frozen": bell_draw(streams_of[8], (TOKENS, WIDTH), 1.0, 6.0, ((0, 4), (1, 8))),
    }


def reference(task_ids, embed_table, trunk_weight, trunk_bias, head_weight, head_bias, token_row, inputs, frozen):
    one_hot = (task_ids[:, None] == jnp.arange(TABLE, dtype=jnp.int32)[None, :]).astype(jnp.bfloat16)
    embedded = jnp.dot(one_hot, embed_table, preferred_element_type=jnp.float32).astype(jnp.bfloat16)
    preact = jnp.dot(embedded, trunk_weight, preferred_element_type=jnp.float32) + trunk_bias
    hidden = jax.nn.silu(preact).astype(jnp.bfloat16)
    factors = (jnp.dot(hidden, head_weight, preferred_element_type=jnp.float32) + head_bias).astype(jnp.bfloat16)
    slice_width = WIDTH // N_WIDTH
    grouped = factors.reshape(ROWS, 2, RANK, slice_width, N_WIDTH).transpose(0, 1, 2, 4, 3).reshape(ROWS, 2, RANK, WIDTH)
    entry_all = grouped[:, 0]
    exit_all = grouped[:, 1]
    inv_width = 1.0 / math.sqrt(WIDTH)
    inv_rank = 1.0 / math.sqrt(RANK)
    block_size = TOK_ROW * math.gcd(ROWS_DEV, 8)
    block_total = TOKENS // block_size

    def adapt_block(block_data):
        tokens_in, frozen_in, rows_in = block_data
        entry_tok = entry_all[rows_in].astype(jnp.float32)
        exit_tok = exit_all[rows_in].astype(jnp.float32)
        coef = jnp.einsum('te,tre->tr', tokens_in.astype(jnp.float32), entry_tok, precision=lax.Precision.HIGHEST)
        coef = (coef * inv_width).astype(jnp.bfloat16)
        update = jnp.einsum('tr,tre->te', coef.astype(jnp.float32), exit_tok, precision=lax.Precision.HIGHEST)
        return (frozen_in.astype(jnp.float32) + update * inv_rank).astype(jnp.bfloat16)
    result = lax.map(adapt_block, (inputs.reshape(block_total, block_size, WIDTH), frozen.reshape(block_total, block_size, WIDTH), token_row.reshape(block_total, block_size)))
    return result.reshape(TOKENS, WIDTH)
```

```python
import functools
import math

import jax
import jax.numpy as jnp
from jax import lax
from jax.experimental import pallas as pl
from jax.experimental.pallas import tpu as pltpu
from jax.sharding import PartitionSpec as P

WIDTH = 8192
RANK = 16
MESH = pl.DeviceIdType.MESH
F32 = jnp.float32
BF16 = jnp.bfloat16


def exchange_kernel(
    dims,
    ids_ref,
    table_hbm,
    trunk_hbm,
    trunk_bias_ref,
    head_hbm,
    head_bias_ref,
    token_ref,
    inputs_hbm,
    factors,
    coef_out,
    ids_all,
    table,
    trunk,
    one_hot,
    hidden,
    weight,
    perm,
    flat,
    outgoing,
    stage,
    entry,
    tokens,
    part,
    gathered,
    coef_all,
    ids_send,
    ids_recv,
    hop_send,
    hop_recv,
    wide_send,
    wide_recv,
    part_send,
    part_recv,
    coef_send,
    coef_recv,
    load_sem,
    weight_sem,
    token_sem,
):
    task_count, width_count, rows, inner, slice_width, step_cols, steps, block = dims
    cols = step_cols * width_count
    task = lax.axis_index("task")
    wide = lax.axis_index("width")
    entry_tasks = [t for t in range(task_count) if t * width_count * inner < RANK * slice_width]
    exit_tasks = [t for t in range(task_count) if t not in entry_tasks]

    def weight_copy(step):
        return pltpu.make_async_copy(
            head_hbm.at[:, pl.ds(pl.multiple_of(step * cols, cols), cols)],
            weight.at[lax.rem(step, weight.shape[0])],
            weight_sem.at[lax.rem(step, weight.shape[0])],
        )

    def token_copy(index):
        return pltpu.make_async_copy(
            inputs_hbm.at[pl.ds(pl.multiple_of(index * block, block), block)],
            tokens.at[lax.rem(index, 2)],
            token_sem.at[lax.rem(index, 2)],
        )

    table_copy = pltpu.make_async_copy(table_hbm, table, load_sem.at[0])
    trunk_copy = pltpu.make_async_copy(trunk_hbm, trunk, load_sem.at[1])
    table_copy.start()
    trunk_copy.start()
    weight_copy(0).start()

    barrier = pltpu.get_barrier_semaphore()
    for d in range(1, task_count):
        pl.semaphore_signal(
            barrier,
            inc=1,
            device_id=(lax.rem(task + d, task_count), wide),
            device_id_type=MESH,
        )
    for d in range(1, width_count):
        pl.semaphore_signal(
            barrier,
            inc=1,
            device_id=(task, lax.rem(wide + d, width_count)),
            device_id_type=MESH,
        )

    ids_all[task] = jnp.broadcast_to(ids_ref[...], (8, rows))
    place = lax.broadcasted_iota(jnp.int32, (1, cols), 1)
    source = (place % step_cols) * width_count + place // step_cols
    for top in range(0, cols, 256):
        down = lax.broadcasted_iota(jnp.int32, (256, cols), 0) + top
        perm[top : top + 256, :] = jnp.where(down == source, 1.0, 0.0).astype(BF16)

    pl.semaphore_wait(barrier, task_count + width_count - 2)

    def ids_copy(peer, slot):
        return pltpu.make_async_remote_copy(
            src_ref=ids_all.at[slot],
            dst_ref=ids_all.at[slot],
            send_sem=ids_send.at[peer],
            recv_sem=ids_recv.at[slot],
            device_id=(peer, wide),
            device_id_type=MESH,
        )

    for d in range(1, task_count):
        ids_copy(lax.rem(task + d, task_count), task).start()
    for d in range(1, task_count):
        ids_copy(lax.rem(task + d, task_count), lax.rem(task + d, task_count)).wait_recv()
    for d in range(1, task_count):
        ids_copy(lax.rem(task + d, task_count), task).wait_send()

    table_len = table.shape[0]
    for t in range(task_count):
        spread_ids = jnp.transpose(jnp.broadcast_to(ids_all[t, 0:1, :], (128, rows)))
        lane = lax.broadcasted_iota(jnp.int32, (rows, 128), 1)
        for k in range(0, table_len, 128):
            one_hot[t * rows : (t + 1) * rows, k : k + 128] = jnp.where(
                spread_ids == lane + k, 1.0, 0.0
            ).astype(BF16)
    table_copy.wait()
    embedded = jnp.dot(one_hot[...], table[...], preferred_element_type=F32).astype(BF16)
    trunk_copy.wait()
    tile = 512
    for k in range(0, trunk.shape[1], tile):
        pre = (
            jnp.dot(embedded, trunk[:, k : k + tile], preferred_element_type=F32)
            + trunk_bias_ref[:, k : k + tile]
        )
        hidden[:, k : k + tile] = (pre / (1.0 + jnp.exp(-pre))).astype(BF16)

    def target(source_task, source_wide, step):
        place = (source_task * width_count + source_wide) * inner + step * step_cols
        return factors.at[
            place // slice_width,
            :,
            pl.ds(pl.multiple_of(lax.rem(place, slice_width), step_cols), step_cols),
        ]

    def hop_copy(peer, source_task, step):
        return pltpu.make_async_remote_copy(
            src_ref=outgoing.at[step, peer],
            dst_ref=stage.at[source_task, step],
            send_sem=hop_send.at[peer, step],
            recv_sem=hop_recv.at[source_task, step],
            device_id=(peer, wide),
            device_id_type=MESH,
        )

    def send_wide(blocks, source_task, step):
        for d in range(1, width_count):
            peer = lax.rem(wide + d, width_count)
            pltpu.make_async_remote_copy(
                src_ref=blocks.at[peer],
                dst_ref=target(source_task, wide, step),
                send_sem=wide_send.at[source_task, step],
                recv_sem=wide_recv.at[source_task, step],
                device_id=(task, peer),
                device_id_type=MESH,
            ).start()
        pltpu.make_async_copy(
            blocks.at[wide], target(source_task, wide, step), wide_recv.at[source_task, step]
        ).start()

    def head_step(step, carry):
        weight_copy(step).wait()

        @pl.when(step + 1 < steps)
        def _():
            weight_copy(step + 1).start()

        slot = lax.rem(step, weight.shape[0])
        for k in range(0, cols, 256):
            total = jnp.dot(
                hidden[...], weight[slot, :, k : k + 256], preferred_element_type=F32
            )
            flat[:, k : k + 256] = (total + head_bias_ref[step, :, k : k + 256]).astype(BF16)
        for k in range(0, cols, 256):
            sorted_cols = jnp.dot(
                flat[...], perm[:, k : k + 256], preferred_element_type=F32
            ).astype(BF16)
            for s in range(0, 256, step_cols):
                for t in range(task_count):
                    outgoing[step, t, (k + s) // step_cols] = sorted_cols[
                        t * rows : (t + 1) * rows, s : s + step_cols
                    ]
        for d in range(1, task_count):
            hop_copy(lax.rem(task + d, task_count), task, step).start()
        send_wide(outgoing.at[step, task], task, step)
        return carry

    lax.fori_loop(0, steps, head_step, 0)
    token_copy(0).start()

    def forward(sources):
        def body(step, carry):
            for t in sources:

                @pl.when(task != t)
                def _():
                    hop_copy(t, t, step).wait_recv()
                    send_wide(stage.at[t, step], t, step)

            return carry

        lax.fori_loop(0, steps, body, 0)

    forward(entry_tasks)
    forward(exit_tasks)

    def wait_wide(sources):
        def body(step, carry):
            for t in sources:
                whole = stage.at[t, step]
                pltpu.make_async_copy(whole, whole, wide_recv.at[t, step]).wait()
            return carry

        lax.fori_loop(0, steps, body, 0)

    wait_wide(entry_tasks)
    entry_copy = pltpu.make_async_copy(factors.at[pl.ds(0, RANK)], entry, load_sem.at[0])
    entry_copy.start()
    entry_copy.wait()

    def part_copy(peer, slot):
        return pltpu.make_async_remote_copy(
            src_ref=part.at[peer],
            dst_ref=gathered.at[slot],
            send_sem=part_send.at[peer],
            recv_sem=part_recv.at[slot],
            device_id=(task, peer),
            device_id_type=MESH,
        )

    def score_block(index, carry):
        token_copy(index).wait()

        @pl.when(index + 1 < width_count)
        def _():
            token_copy(index + 1).start()

        local = token_ref[index] - task * rows
        chosen = lax.broadcasted_iota(jnp.int32, (rows, block), 0) == local
        block_in = tokens[lax.rem(index, 2)]
        half = RANK // 2
        for top in range(0, RANK, half):
            scores = lax.dot_general(
                entry[top : top + half].reshape(half * rows, slice_width),
                block_in,
                (((1,), (1,)), ((), ())),
                preferred_element_type=F32,
            ).reshape(half, rows, block)
            part[index, top : top + half] = jnp.sum(
                jnp.where(chosen[None], scores, 0.0), axis=1
            )

        @pl.when(index != wide)
        def _():
            part_copy(index, wide).start()

        return carry

    lax.fori_loop(0, width_count, score_block, 0)
    total = part[wide]
    for d in range(1, width_count):
        peer = lax.rem(wide + d, width_count)
        part_copy(peer, peer).wait_recv()
        total = total + gathered[peer]
    coef_all[wide] = (total * (1.0 / math.sqrt(WIDTH))).astype(BF16)

    def coef_copy(peer, slot):
        return pltpu.make_async_remote_copy(
            src_ref=coef_all.at[slot],
            dst_ref=coef_all.at[slot],
            send_sem=coef_send.at[peer],
            recv_sem=coef_recv.at[slot],
            device_id=(task, peer),
            device_id_type=MESH,
        )

    for d in range(1, width_count):
        coef_copy(lax.rem(wide + d, width_count), wide).start()
    for d in range(1, width_count):
        peer = lax.rem(wide + d, width_count)
        coef_copy(peer, peer).wait_recv()
    coef_out[...] = coef_all[...]

    for d in range(1, width_count):
        peer = lax.rem(wide + d, width_count)
        part_copy(peer, peer).wait_send()
        coef_copy(peer, wide).wait_send()

    def drain(step, carry):
        for d in range(1, task_count):
            hop_copy(lax.rem(task + d, task_count), task, step).wait_send()
        for t in range(task_count):
            sent = stage.at[t, step, pl.ds(0, width_count - 1)]
            pltpu.make_async_copy(sent, sent, wide_send.at[t, step]).wait()
        return carry

    lax.fori_loop(0, steps, drain, 0)
    wait_wide(exit_tasks)


def update_kernel(rows, token_ref, coef_ref, exit_ref, frozen_ref, out_ref):
    local = token_ref[0] - lax.axis_index("task") * rows
    block = local.shape[1]
    spread_ids = jnp.transpose(jnp.broadcast_to(local, (128, block)))
    chosen = spread_ids == lax.broadcasted_iota(jnp.int32, (block, 128), 1)
    coef = jnp.transpose(coef_ref[0].astype(F32))
    spread = jnp.concatenate(
        [jnp.where(chosen, coef[:, r : r + 1], 0.0).astype(BF16)[:, :rows] for r in range(RANK)],
        axis=1,
    )
    exit_flat = exit_ref[...].reshape(RANK * rows, exit_ref.shape[2])
    tile = min(512, exit_ref.shape[2])
    for k in range(0, exit_ref.shape[2], tile):
        update = jnp.dot(spread, exit_flat[:, k : k + tile], preferred_element_type=F32)
        out_ref[:, k : k + tile] = (
            frozen_ref[:, k : k + tile].astype(F32) + update * (1.0 / math.sqrt(RANK))
        ).astype(BF16)


def on_device(
    task_ids,
    embed_table,
    trunk_weight,
    trunk_bias,
    head_weight,
    head_bias,
    token_row,
    inputs,
    frozen,
):
    task_count = lax.axis_size("task")
    width_count = lax.axis_size("width")
    rows = task_ids.shape[0]
    hid = trunk_weight.shape[1]
    inner = head_weight.shape[1] // width_count
    tok_count, slice_width = inputs.shape
    step_cols = 128
    steps = inner // step_cols
    cols = step_cols * width_count
    block = tok_count // width_count
    dims = (task_count, width_count, rows, inner, slice_width, step_cols, steps, block)
    all_rows = task_count * rows
    token_blocks = token_row.reshape(width_count, 1, block)
    vmem = pl.BlockSpec(memory_space=pltpu.VMEM)
    hbm = pl.BlockSpec(memory_space=pl.ANY)
    dma = pltpu.SemaphoreType.DMA
    factors, coef = pl.pallas_call(
        functools.partial(exchange_kernel, dims),
        out_shape=(
            jax.ShapeDtypeStruct((2 * RANK, rows, slice_width), BF16),
            jax.ShapeDtypeStruct((width_count, RANK, block), BF16),
        ),
        in_specs=[vmem, hbm, hbm, vmem, hbm, vmem, vmem, hbm],
        out_specs=(hbm, vmem),
        scratch_shapes=[
            pltpu.VMEM((task_count, 8, rows), jnp.int32),
            pltpu.VMEM(embed_table.shape, BF16),
            pltpu.VMEM(trunk_weight.shape, BF16),
            pltpu.VMEM((all_rows, embed_table.shape[0]), BF16),
            pltpu.VMEM((all_rows, hid), BF16),
            pltpu.VMEM((min(2, steps), hid, cols), BF16),
            pltpu.VMEM((cols, cols), BF16),
            pltpu.VMEM((all_rows, cols), BF16),
            pltpu.VMEM((steps, task_count, width_count, rows, step_cols), BF16),
            pltpu.VMEM((task_count, steps, width_count, rows, step_cols), BF16),
            pltpu.VMEM((RANK, rows, slice_width), BF16),
            pltpu.VMEM((2, block, slice_width), BF16),
            pltpu.VMEM((width_count, RANK, block), F32),
            pltpu.VMEM((width_count, RANK, block), F32),
            pltpu.VMEM((width_count, RANK, block), BF16),
            dma((task_count,)),
            dma((task_count,)),
            dma((task_count, steps)),
            dma((task_count, steps)),
            dma((task_count, steps)),
            dma((task_count, steps)),
            dma((width_count,)),
            dma((width_count,)),
            dma((width_count,)),
            dma((width_count,)),
            dma((2,)),
            dma((2,)),
            dma((2,)),
        ],
        compiler_params=pltpu.CompilerParams(
            collective_id=0, has_side_effects=True, vmem_limit_bytes=58 * 1024 * 1024
        ),
        name="factor_exchange",
    )(
        task_ids.reshape(1, rows),
        embed_table,
        trunk_weight,
        trunk_bias.reshape(1, hid),
        head_weight,
        head_bias.reshape(steps, 1, cols),
        token_blocks,
        inputs,
    )
    return pl.pallas_call(
        functools.partial(update_kernel, rows),
        grid=(width_count,),
        out_shape=jax.ShapeDtypeStruct((tok_count, slice_width), BF16),
        in_specs=[
            pl.BlockSpec((1, 1, block), lambda i: (i, 0, 0)),
            pl.BlockSpec((1, RANK, block), lambda i: (i, 0, 0)),
            pl.BlockSpec((RANK, rows, slice_width), lambda i: (1, 0, 0)),
            pl.BlockSpec((block, slice_width), lambda i: (i, 0)),
        ],
        out_specs=pl.BlockSpec((block, slice_width), lambda i: (i, 0)),
        compiler_params=pltpu.CompilerParams(vmem_limit_bytes=48 * 1024 * 1024),
        name="apply_update",
    )(token_blocks, coef, factors, frozen)


def solution(mesh):
    return jax.shard_map(
        on_device,
        mesh=mesh,
        in_specs=(
            P("task"),
            P(),
            P(),
            P(),
            P(None, ("task", "width")),
            P(("task", "width")),
            P("task"),
            P("task", "width"),
            P("task", "width"),
        ),
        out_specs=P("task", "width"),
        check_vma=False,
    )
```

```python
import functools
import math

import jax
import jax.numpy as jnp
from jax import lax
from jax.experimental import pallas as pl
from jax.experimental.pallas import tpu as pltpu
from jax.sharding import PartitionSpec as P

WIDTH = 8192
RANK = 16
MESH = pl.DeviceIdType.MESH
F32 = jnp.float32
BF16 = jnp.bfloat16


def exchange_kernel(
    dims,
    ids_ref,
    table_hbm,
    trunk_hbm,
    trunk_bias_ref,
    head_hbm,
    head_bias_ref,
    token_ref,
    inputs_hbm,
    frozen_hbm,
    out_hbm,
    factors,
    ids_all,
    outgoing,
    stage,
    part,
    gathered,
    coef_all,
    ids_send,
    ids_recv,
    hop_send,
    hop_recv,
    wide_send,
    wide_recv,
    part_send,
    part_recv,
    coef_send,
    coef_recv,
    load_sem,
    weight_sem,
    token_sem,
    frozen_sem,
    out_sem,
):
    task_count, width_count, rows, inner, slice_width, step_cols, steps, block = dims
    cols = step_cols * width_count
    task = lax.axis_index("task")
    wide = lax.axis_index("width")
    entry_tasks = [t for t in range(task_count) if t * width_count * inner < RANK * slice_width]
    exit_tasks = [t for t in range(task_count) if t not in entry_tasks]

    hid = trunk_hbm.shape[1]
    all_rows = task_count * rows

    def partner(distance):
        if width_count & (width_count - 1):
            return lax.rem(wide + distance, width_count)
        peer = wide
        for bit in range(width_count.bit_length() - 1):
            if (distance >> bit) & 1:
                peer = peer + (1 << bit) * (1 - 2 * lax.rem(wide // (1 << bit), 2))
        return peer

    def target(source_task, source_wide, step):
        place = (source_task * width_count + source_wide) * inner + step * step_cols
        return factors.at[
            place // slice_width,
            :,
            pl.ds(pl.multiple_of(lax.rem(place, slice_width), step_cols), step_cols),
        ]

    def hop_copy(peer, source_task, step):
        return pltpu.make_async_remote_copy(
            src_ref=outgoing.at[step, peer],
            dst_ref=stage.at[source_task, step],
            send_sem=hop_send.at[peer, step],
            recv_sem=hop_recv.at[source_task, step],
            device_id=(peer, wide),
            device_id_type=MESH,
        )

    def send_wide(blocks, source_task, step):
        for d in reversed(range(1, width_count)):
            peer = partner(d)
            pltpu.make_async_remote_copy(
                src_ref=blocks.at[peer],
                dst_ref=target(source_task, wide, step),
                send_sem=wide_send.at[source_task, step],
                recv_sem=wide_recv.at[source_task, step],
                device_id=(task, peer),
                device_id_type=MESH,
            ).start()
        pltpu.make_async_copy(
            blocks.at[wide], target(source_task, wide, step), wide_recv.at[source_task, step]
        ).start()

    def forward(sources, step):
        for t in sources:

            @pl.when(task != t)
            def _():
                hop_copy(t, t, step).wait_recv()
                send_wide(stage.at[t, step], t, step)

    def forward_all(sources, first):
        def body(step, carry):
            forward(sources, step)
            return carry

        lax.fori_loop(first, steps, body, 0)

    def wait_wide(sources, step):
        for t in sources:
            whole = stage.at[t, step]
            pltpu.make_async_copy(whole, whole, wide_recv.at[t, step]).wait()

    def wait_wide_all(sources):
        def body(step, carry):
            wait_wide(sources, step)
            return carry

        lax.fori_loop(0, steps, body, 0)

    lag = 5
    early = max(0, steps - lag)

    def generate(table, trunk, one_hot, hidden, weight, perm, flat):
        def weight_copy(step):
            return pltpu.make_async_copy(
                head_hbm.at[:, pl.ds(pl.multiple_of(step * cols, cols), cols)],
                weight.at[lax.rem(step, weight.shape[0])],
                weight_sem.at[lax.rem(step, weight.shape[0])],
            )

        table_copy = pltpu.make_async_copy(table_hbm, table, load_sem.at[0])
        trunk_copy = pltpu.make_async_copy(trunk_hbm, trunk, load_sem.at[1])
        table_copy.start()
        trunk_copy.start()
        weight_copy(0).start()

        barrier = pltpu.get_barrier_semaphore()
        for d in range(1, task_count):
            pl.semaphore_signal(
                barrier,
                inc=1,
                device_id=(lax.rem(task + d, task_count), wide),
                device_id_type=MESH,
            )
        for d in range(1, width_count):
            pl.semaphore_signal(
                barrier,
                inc=1,
                device_id=(task, lax.rem(wide + d, width_count)),
                device_id_type=MESH,
            )

        ids_all[task] = jnp.broadcast_to(ids_ref[...], (8, rows))
        place = lax.broadcasted_iota(jnp.int32, (1, cols), 1)
        source = (place % step_cols) * width_count + place // step_cols
        for top in range(0, cols, 256):
            down = lax.broadcasted_iota(jnp.int32, (256, cols), 0) + top
            perm[top : top + 256, :] = jnp.where(down == source, 1.0, 0.0).astype(BF16)

        pl.semaphore_wait(barrier, task_count + width_count - 2)

        def ids_copy(peer, slot):
            return pltpu.make_async_remote_copy(
                src_ref=ids_all.at[slot],
                dst_ref=ids_all.at[slot],
                send_sem=ids_send.at[peer],
                recv_sem=ids_recv.at[slot],
                device_id=(peer, wide),
                device_id_type=MESH,
            )

        for d in range(1, task_count):
            ids_copy(lax.rem(task + d, task_count), task).start()
        for d in range(1, task_count):
            ids_copy(lax.rem(task + d, task_count), lax.rem(task + d, task_count)).wait_recv()
        for d in range(1, task_count):
            ids_copy(lax.rem(task + d, task_count), task).wait_send()

        table_len = table.shape[0]
        for t in range(task_count):
            spread_ids = jnp.transpose(jnp.broadcast_to(ids_all[t, 0:1, :], (128, rows)))
            lane = lax.broadcasted_iota(jnp.int32, (rows, 128), 1)
            for k in range(0, table_len, 128):
                one_hot[t * rows : (t + 1) * rows, k : k + 128] = jnp.where(
                    spread_ids == lane + k, 1.0, 0.0
                ).astype(BF16)
        table_copy.wait()
        embedded = jnp.dot(one_hot[...], table[...], preferred_element_type=F32).astype(BF16)
        trunk_copy.wait()
        tile = 512
        for k in range(0, trunk.shape[1], tile):
            pre = (
                jnp.dot(embedded, trunk[:, k : k + tile], preferred_element_type=F32)
                + trunk_bias_ref[:, k : k + tile]
            )
            hidden[:, k : k + tile] = (pre / (1.0 + jnp.exp(-pre))).astype(BF16)

        def head_step(step, carry):
            weight_copy(step).wait()

            @pl.when(step + 1 < steps)
            def _():
                weight_copy(step + 1).start()

            slot = lax.rem(step, weight.shape[0])
            for k in range(0, cols, 256):
                total = jnp.dot(
                    hidden[...], weight[slot, :, k : k + 256], preferred_element_type=F32
                )
                flat[:, k : k + 256] = (total + head_bias_ref[step, :, k : k + 256]).astype(BF16)
            for k in range(0, cols, 256):
                sorted_cols = jnp.dot(
                    flat[...], perm[:, k : k + 256], preferred_element_type=F32
                ).astype(BF16)
                for s in range(0, 256, step_cols):
                    for t in range(task_count):
                        outgoing[step, t, (k + s) // step_cols] = sorted_cols[
                            t * rows : (t + 1) * rows, s : s + step_cols
                        ]
            for d in range(1, task_count):
                hop_copy(lax.rem(task + d, task_count), task, step).start()
            send_wide(outgoing.at[step, task], task, step)
            if early:

                @pl.when(step >= lag)
                def _():
                    forward(entry_tasks, step - lag)

            return carry

        lax.fori_loop(0, steps, head_step, 0)

    pl.run_scoped(
        generate,
        pltpu.VMEM(table_hbm.shape, BF16),
        pltpu.VMEM(trunk_hbm.shape, BF16),
        pltpu.VMEM((all_rows, table_hbm.shape[0]), BF16),
        pltpu.VMEM((all_rows, hid), BF16),
        pltpu.VMEM((min(2, steps), hid, cols), BF16),
        pltpu.VMEM((cols, cols), BF16),
        pltpu.VMEM((all_rows, cols), BF16),
    )
    forward_all(entry_tasks, early)
    forward_all(exit_tasks, 0)
    wait_wide_all(entry_tasks)

    def part_copy(peer, slot):
        return pltpu.make_async_remote_copy(
            src_ref=part.at[peer],
            dst_ref=gathered.at[slot],
            send_sem=part_send.at[peer],
            recv_sem=part_recv.at[slot],
            device_id=(task, peer),
            device_id_type=MESH,
        )

    def rank(entry, tokens):
        def token_copy(index):
            return pltpu.make_async_copy(
                inputs_hbm.at[pl.ds(pl.multiple_of(index * block, block), block)],
                tokens.at[lax.rem(index, 2)],
                token_sem.at[lax.rem(index, 2)],
            )

        token_copy(0).start()
        entry_copy = pltpu.make_async_copy(factors.at[pl.ds(0, RANK)], entry, load_sem.at[0])
        entry_copy.start()
        entry_copy.wait()

        def score_block(index, carry):
            token_copy(index).wait()

            @pl.when(index + 1 < width_count)
            def _():
                token_copy(index + 1).start()

            local = token_ref[index] - task * rows
            chosen = lax.broadcasted_iota(jnp.int32, (rows, block), 0) == local
            block_in = tokens[lax.rem(index, 2)]
            half = RANK // 2
            for top in range(0, RANK, half):
                scores = lax.dot_general(
                    entry[top : top + half].reshape(half * rows, slice_width),
                    block_in,
                    (((1,), (1,)), ((), ())),
                    preferred_element_type=F32,
                ).reshape(half, rows, block)
                part[index, top : top + half] = jnp.sum(
                    jnp.where(chosen[None], scores, 0.0), axis=1
                )

            @pl.when(index != wide)
            def _():
                part_copy(index, wide).start()

            return carry

        lax.fori_loop(0, width_count, score_block, 0)

    pl.run_scoped(
        rank,
        pltpu.VMEM((RANK, rows, slice_width), BF16),
        pltpu.VMEM((2, block, slice_width), BF16),
    )
    total = part[wide]
    for d in range(1, width_count):
        peer = lax.rem(wide + d, width_count)
        part_copy(peer, peer).wait_recv()
        total = total + gathered[peer]
    coef_all[wide] = (total * (1.0 / math.sqrt(WIDTH))).astype(BF16)

    def coef_copy(peer, slot):
        return pltpu.make_async_remote_copy(
            src_ref=coef_all.at[slot],
            dst_ref=coef_all.at[slot],
            send_sem=coef_send.at[peer],
            recv_sem=coef_recv.at[slot],
            device_id=(task, peer),
            device_id_type=MESH,
        )

    for d in range(1, width_count):
        coef_copy(lax.rem(wide + d, width_count), wide).start()
    for d in range(1, width_count):
        peer = lax.rem(wide + d, width_count)
        coef_copy(peer, peer).wait_recv()
    chunk = min(256, slice_width)
    aligned = inner % slice_width == 0 and chunk % step_cols == 0

    def update(spread, exit_buf, frozen_buf, out_buf):
        def columns(array, index):
            return array.at[:, pl.ds(pl.multiple_of(index * chunk, chunk), chunk)]

        def frozen_copy(index):
            slot = lax.rem(index, 2)
            return pltpu.make_async_copy(
                columns(frozen_hbm, index), frozen_buf.at[slot], frozen_sem.at[slot]
            )

        def out_copy(index):
            slot = lax.rem(index, 2)
            return pltpu.make_async_copy(
                out_buf.at[slot], columns(out_hbm, index), out_sem.at[slot]
            )

        frozen_copy(0).start()

        def spread_block(index, carry):
            local = token_ref[index] - task * rows
            spread_ids = jnp.transpose(jnp.broadcast_to(local, (128, block)))
            chosen = spread_ids == lax.broadcasted_iota(jnp.int32, (block, 128), 1)
            coef = jnp.transpose(coef_all[index].astype(F32))
            place = pl.ds(pl.multiple_of(index * block, block), block)
            for r in range(RANK):
                piece = jnp.where(chosen, coef[:, r : r + 1], 0.0).astype(BF16)
                spread[place, r * rows : (r + 1) * rows] = piece[:, :rows]
            return carry

        lax.fori_loop(0, width_count, spread_block, 0)
        count = slice_width // chunk
        if not aligned:
            wait_wide_all(exit_tasks)

        def update_chunk(index, carry):
            slot = lax.rem(index, 2)

            @pl.when(index + 1 < count)
            def _():
                frozen_copy(index + 1).start()

            if aligned:
                per = chunk // step_cols
                for turn in range(inner // slice_width):
                    for q in range(per):
                        wait_wide(
                            exit_tasks, turn * (slice_width // step_cols) + index * per + q
                        )
            exit_copy = pltpu.make_async_copy(
                factors.at[
                    pl.ds(RANK, RANK), :, pl.ds(pl.multiple_of(index * chunk, chunk), chunk)
                ],
                exit_buf,
                load_sem.at[1],
            )
            exit_copy.start()
            frozen_copy(index).wait()

            @pl.when(index >= 2)
            def _():
                out_copy(index - 2).wait()

            exit_copy.wait()

            def token_block(row_block, inner_carry):
                place = pl.ds(pl.multiple_of(row_block * block, block), block)
                change = jnp.dot(
                    spread[place, :],
                    exit_buf[...].reshape(RANK * rows, chunk),
                    preferred_element_type=F32,
                )
                out_buf[slot, place, :] = (
                    frozen_buf[slot, place, :].astype(F32) + change * (1.0 / math.sqrt(RANK))
                ).astype(BF16)
                return inner_carry

            lax.fori_loop(0, width_count, token_block, 0)
            out_copy(index).start()
            return carry

        lax.fori_loop(0, count, update_chunk, 0)
        for index in range(max(0, count - 2), count):
            out_copy(index).wait()

    tok_count = width_count * block
    pl.run_scoped(
        update,
        pltpu.VMEM((tok_count, RANK * rows), BF16),
        pltpu.VMEM((RANK, rows, chunk), BF16),
        pltpu.VMEM((2, tok_count, chunk), BF16),
        pltpu.VMEM((2, tok_count, chunk), BF16),
    )

    for d in range(1, width_count):
        peer = lax.rem(wide + d, width_count)
        part_copy(peer, peer).wait_send()
        coef_copy(peer, wide).wait_send()

    def drain(step, carry):
        for d in range(1, task_count):
            hop_copy(lax.rem(task + d, task_count), task, step).wait_send()
        for t in range(task_count):
            sent = stage.at[t, step, pl.ds(0, width_count - 1)]
            pltpu.make_async_copy(sent, sent, wide_send.at[t, step]).wait()
        return carry

    lax.fori_loop(0, steps, drain, 0)


def on_device(
    task_ids,
    embed_table,
    trunk_weight,
    trunk_bias,
    head_weight,
    head_bias,
    token_row,
    inputs,
    frozen,
):
    task_count = lax.axis_size("task")
    width_count = lax.axis_size("width")
    rows = task_ids.shape[0]
    hid = trunk_weight.shape[1]
    inner = head_weight.shape[1] // width_count
    tok_count, slice_width = inputs.shape
    step_cols = 128
    steps = inner // step_cols
    cols = step_cols * width_count
    block = tok_count // width_count
    dims = (task_count, width_count, rows, inner, slice_width, step_cols, steps, block)
    token_blocks = token_row.reshape(width_count, 1, block)
    vmem = pl.BlockSpec(memory_space=pltpu.VMEM)
    hbm = pl.BlockSpec(memory_space=pl.ANY)
    dma = pltpu.SemaphoreType.DMA
    out, _ = pl.pallas_call(
        functools.partial(exchange_kernel, dims),
        out_shape=(
            jax.ShapeDtypeStruct((tok_count, slice_width), BF16),
            jax.ShapeDtypeStruct((2 * RANK, rows, slice_width), BF16),
        ),
        in_specs=[vmem, hbm, hbm, vmem, hbm, vmem, vmem, hbm, hbm],
        out_specs=(hbm, hbm),
        scratch_shapes=[
            pltpu.VMEM((task_count, 8, rows), jnp.int32),
            pltpu.VMEM((steps, task_count, width_count, rows, step_cols), BF16),
            pltpu.VMEM((task_count, steps, width_count, rows, step_cols), BF16),
            pltpu.VMEM((width_count, RANK, block), F32),
            pltpu.VMEM((width_count, RANK, block), F32),
            pltpu.VMEM((width_count, RANK, block), BF16),
            dma((task_count,)),
            dma((task_count,)),
            dma((task_count, steps)),
            dma((task_count, steps)),
            dma((task_count, steps)),
            dma((task_count, steps)),
            dma((width_count,)),
            dma((width_count,)),
            dma((width_count,)),
            dma((width_count,)),
            dma((2,)),
            dma((2,)),
            dma((2,)),
            dma((2,)),
            dma((2,)),
        ],
        compiler_params=pltpu.CompilerParams(
            collective_id=0, has_side_effects=True, vmem_limit_bytes=58 * 1024 * 1024
        ),
        name="adapt_rows",
    )(
        task_ids.reshape(1, rows),
        embed_table,
        trunk_weight,
        trunk_bias.reshape(1, hid),
        head_weight,
        head_bias.reshape(steps, 1, cols),
        token_blocks,
        inputs,
        frozen,
    )
    return out


def solution(mesh):
    return jax.shard_map(
        on_device,
        mesh=mesh,
        in_specs=(
            P("task"),
            P(),
            P(),
            P(),
            P(None, ("task", "width")),
            P(("task", "width")),
            P("task"),
            P("task", "width"),
            P("task", "width"),
        ),
        out_specs=P("task", "width"),
        check_vma=False,
    )
```

```python
import functools
import math

import jax
import jax.numpy as jnp
from jax import lax
from jax.experimental import pallas as pl
from jax.experimental.pallas import tpu as pltpu
from jax.sharding import PartitionSpec as P

WIDTH = 8192
RANK = 16
MESH = pl.DeviceIdType.MESH
F32 = jnp.float32
BF16 = jnp.bfloat16


def exchange_kernel(
    dims,
    ids_ref,
    table_hbm,
    trunk_hbm,
    trunk_bias_ref,
    head_hbm,
    head_bias_ref,
    token_ref,
    inputs_hbm,
    frozen_hbm,
    out_hbm,
    factors,
    ids_all,
    outgoing,
    stage,
    part,
    gathered,
    coef_all,
    ids_send,
    ids_recv,
    hop_send,
    hop_recv,
    wide_send,
    wide_recv,
    part_send,
    part_recv,
    coef_send,
    coef_recv,
    load_sem,
    weight_sem,
    token_sem,
    frozen_sem,
    out_sem,
):
    task_count, width_count, rows, inner, slice_width, step_cols, steps, block = dims
    cols = step_cols * width_count
    task = lax.axis_index("task")
    wide = lax.axis_index("width")
    entry_tasks = [t for t in range(task_count) if t * width_count * inner < RANK * slice_width]
    exit_tasks = [t for t in range(task_count) if t not in entry_tasks]

    hid = trunk_hbm.shape[1]
    all_rows = task_count * rows

    def target(source_task, source_wide, step):
        place = (source_task * width_count + source_wide) * inner + step * step_cols
        return factors.at[
            place // slice_width,
            :,
            pl.ds(pl.multiple_of(lax.rem(place, slice_width), step_cols), step_cols),
        ]

    def hop_copy(peer, source_task, step):
        return pltpu.make_async_remote_copy(
            src_ref=outgoing.at[step, peer],
            dst_ref=stage.at[source_task, step],
            send_sem=hop_send.at[peer, step],
            recv_sem=hop_recv.at[source_task, step],
            device_id=(peer, wide),
            device_id_type=MESH,
        )

    def send_wide(blocks, source_task, step):
        for d in range(1, width_count):
            peer = lax.rem(wide + d, width_count)
            pltpu.make_async_remote_copy(
                src_ref=blocks.at[peer],
                dst_ref=target(source_task, wide, step),
                send_sem=wide_send.at[source_task, step],
                recv_sem=wide_recv.at[source_task, step],
                device_id=(task, peer),
                device_id_type=MESH,
            ).start()
        pltpu.make_async_copy(
            blocks.at[wide], target(source_task, wide, step), wide_recv.at[source_task, step]
        ).start()

    def forward(sources, step):
        for t in sources:

            @pl.when(task != t)
            def _():
                hop_copy(t, t, step).wait_recv()
                send_wide(stage.at[t, step], t, step)

    def wait_sent(sources, step):
        for t in sources:
            sent = stage.at[t, step, pl.ds(0, width_count - 1)]
            pltpu.make_async_copy(sent, sent, wide_send.at[t, step]).wait()

    def forward_entry(step, carry):
        forward(entry_tasks, step)
        return carry

    def forward_exit(step, carry):
        wait_sent(entry_tasks, step)
        forward(exit_tasks, step)
        return carry

    def wait_wide(sources, step):
        for t in sources:
            whole = stage.at[t, step]
            pltpu.make_async_copy(whole, whole, wide_recv.at[t, step]).wait()

    def wait_wide_all(sources):
        def body(step, carry):
            wait_wide(sources, step)
            return carry

        lax.fori_loop(0, steps, body, 0)

    def generate(table, trunk, one_hot, hidden, weight, perm, flat):
        def weight_copy(step):
            return pltpu.make_async_copy(
                head_hbm.at[:, pl.ds(pl.multiple_of(step * cols, cols), cols)],
                weight.at[lax.rem(step, weight.shape[0])],
                weight_sem.at[lax.rem(step, weight.shape[0])],
            )

        table_copy = pltpu.make_async_copy(table_hbm, table, load_sem.at[0])
        trunk_copy = pltpu.make_async_copy(trunk_hbm, trunk, load_sem.at[1])
        table_copy.start()
        trunk_copy.start()
        weight_copy(0).start()

        barrier = pltpu.get_barrier_semaphore()
        for d in range(1, task_count):
            pl.semaphore_signal(
                barrier,
                inc=1,
                device_id=(lax.rem(task + d, task_count), wide),
                device_id_type=MESH,
            )
        for d in range(1, width_count):
            pl.semaphore_signal(
                barrier,
                inc=1,
                device_id=(task, lax.rem(wide + d, width_count)),
                device_id_type=MESH,
            )

        ids_all[task] = jnp.broadcast_to(ids_ref[...], (8, rows))
        place = lax.broadcasted_iota(jnp.int32, (1, cols), 1)
        source = (place % step_cols) * width_count + place // step_cols
        for top in range(0, cols, 256):
            down = lax.broadcasted_iota(jnp.int32, (256, cols), 0) + top
            perm[top : top + 256, :] = jnp.where(down == source, 1.0, 0.0).astype(BF16)

        pl.semaphore_wait(barrier, task_count + width_count - 2)

        def ids_copy(peer, slot):
            return pltpu.make_async_remote_copy(
                src_ref=ids_all.at[slot],
                dst_ref=ids_all.at[slot],
                send_sem=ids_send.at[peer],
                recv_sem=ids_recv.at[slot],
                device_id=(peer, wide),
                device_id_type=MESH,
            )

        for d in range(1, task_count):
            ids_copy(lax.rem(task + d, task_count), task).start()
        for d in range(1, task_count):
            ids_copy(lax.rem(task + d, task_count), lax.rem(task + d, task_count)).wait_recv()
        for d in range(1, task_count):
            ids_copy(lax.rem(task + d, task_count), task).wait_send()

        table_len = table.shape[0]
        for t in range(task_count):
            spread_ids = jnp.transpose(jnp.broadcast_to(ids_all[t, 0:1, :], (128, rows)))
            lane = lax.broadcasted_iota(jnp.int32, (rows, 128), 1)
            for k in range(0, table_len, 128):
                one_hot[t * rows : (t + 1) * rows, k : k + 128] = jnp.where(
                    spread_ids == lane + k, 1.0, 0.0
                ).astype(BF16)
        table_copy.wait()
        embedded = jnp.dot(one_hot[...], table[...], preferred_element_type=F32).astype(BF16)
        trunk_copy.wait()
        tile = 512
        for k in range(0, trunk.shape[1], tile):
            pre = (
                jnp.dot(embedded, trunk[:, k : k + tile], preferred_element_type=F32)
                + trunk_bias_ref[:, k : k + tile]
            )
            hidden[:, k : k + tile] = (pre / (1.0 + jnp.exp(-pre))).astype(BF16)

        def head_step(step, carry):
            weight_copy(step).wait()

            @pl.when(step + 1 < steps)
            def _():
                weight_copy(step + 1).start()

            slot = lax.rem(step, weight.shape[0])
            for k in range(0, cols, 256):
                total = jnp.dot(
                    hidden[...], weight[slot, :, k : k + 256], preferred_element_type=F32
                )
                flat[:, k : k + 256] = (total + head_bias_ref[step, :, k : k + 256]).astype(BF16)
            for k in range(0, cols, 256):
                sorted_cols = jnp.dot(
                    flat[...], perm[:, k : k + 256], preferred_element_type=F32
                ).astype(BF16)
                for s in range(0, 256, step_cols):
                    for t in range(task_count):
                        outgoing[step, t, (k + s) // step_cols] = sorted_cols[
                            t * rows : (t + 1) * rows, s : s + step_cols
                        ]
            for d in range(1, task_count):
                hop_copy(lax.rem(task + d, task_count), task, step).start()
            send_wide(outgoing.at[step, task], task, step)
            return carry

        lax.fori_loop(0, steps, head_step, 0)

    pl.run_scoped(
        generate,
        pltpu.VMEM(table_hbm.shape, BF16),
        pltpu.VMEM(trunk_hbm.shape, BF16),
        pltpu.VMEM((all_rows, table_hbm.shape[0]), BF16),
        pltpu.VMEM((all_rows, hid), BF16),
        pltpu.VMEM((min(2, steps), hid, cols), BF16),
        pltpu.VMEM((cols, cols), BF16),
        pltpu.VMEM((all_rows, cols), BF16),
    )
    lax.fori_loop(0, steps, forward_entry, 0)
    lax.fori_loop(0, steps, forward_exit, 0)

    chunk = min(256, slice_width)
    aligned = inner % slice_width == 0 and chunk % step_cols == 0
    count = slice_width // chunk

    def columns(array, index):
        return array.at[:, pl.ds(pl.multiple_of(index * chunk, chunk), chunk)]

    def factor_columns(first, index):
        return factors.at[
            pl.ds(first, RANK), :, pl.ds(pl.multiple_of(index * chunk, chunk), chunk)
        ]

    def wait_columns(sources, index):
        per = chunk // step_cols
        for turn in range(inner // slice_width):
            for q in range(per):
                wait_wide(sources, turn * (slice_width // step_cols) + index * per + q)

    def part_copy(peer, slot):
        return pltpu.make_async_remote_copy(
            src_ref=part.at[peer],
            dst_ref=gathered.at[slot],
            send_sem=part_send.at[peer],
            recv_sem=part_recv.at[slot],
            device_id=(task, peer),
            device_id_type=MESH,
        )

    def rank(entry, tokens):
        def token_copy(index):
            slot = lax.rem(index, 2)
            return pltpu.make_async_copy(
                columns(inputs_hbm, index), tokens.at[slot], token_sem.at[slot]
            )

        token_copy(0).start()
        part[...] = jnp.zeros_like(part)
        if not aligned:
            wait_wide_all(entry_tasks)

        def score_piece(index, carry):
            slot = lax.rem(index, 2)

            @pl.when(index + 1 < count)
            def _():
                token_copy(index + 1).start()

            if aligned:
                wait_columns(entry_tasks, index)
            entry_copy = pltpu.make_async_copy(factor_columns(0, index), entry, load_sem.at[0])
            entry_copy.start()
            token_copy(index).wait()
            entry_copy.wait()

            def score_block(row_block, inner_carry):
                local = token_ref[row_block] - task * rows
                chosen = lax.broadcasted_iota(jnp.int32, (rows, block), 0) == local
                place = pl.ds(pl.multiple_of(row_block * block, block), block)
                block_in = tokens[slot, place, :]
                half = RANK // 2
                for top in range(0, RANK, half):
                    scores = lax.dot_general(
                        entry[top : top + half].reshape(half * rows, chunk),
                        block_in,
                        (((1,), (1,)), ((), ())),
                        preferred_element_type=F32,
                    ).reshape(half, rows, block)
                    part[row_block, top : top + half] += jnp.sum(
                        jnp.where(chosen[None], scores, 0.0), axis=1
                    )

                @pl.when(jnp.logical_and(index == count - 1, row_block != wide))
                def _():
                    part_copy(row_block, wide).start()

                return inner_carry

            lax.fori_loop(0, width_count, score_block, 0)
            return carry

        lax.fori_loop(0, count, score_piece, 0)

    pl.run_scoped(
        rank,
        pltpu.VMEM((RANK, rows, chunk), BF16),
        pltpu.VMEM((2, width_count * block, chunk), BF16),
    )
    total = part[wide]
    for d in range(1, width_count):
        peer = lax.rem(wide + d, width_count)
        part_copy(peer, peer).wait_recv()
        total = total + gathered[peer]
    coef_all[wide] = (total * (1.0 / math.sqrt(WIDTH))).astype(BF16)

    def coef_copy(peer, slot):
        return pltpu.make_async_remote_copy(
            src_ref=coef_all.at[slot],
            dst_ref=coef_all.at[slot],
            send_sem=coef_send.at[peer],
            recv_sem=coef_recv.at[slot],
            device_id=(task, peer),
            device_id_type=MESH,
        )

    for d in range(1, width_count):
        coef_copy(lax.rem(wide + d, width_count), wide).start()
    for d in range(1, width_count):
        peer = lax.rem(wide + d, width_count)
        coef_copy(peer, peer).wait_recv()
    def update(spread, exit_buf, frozen_buf, out_buf):
        def frozen_copy(index):
            slot = lax.rem(index, 2)
            return pltpu.make_async_copy(
                columns(frozen_hbm, index), frozen_buf.at[slot], frozen_sem.at[slot]
            )

        def out_copy(index):
            slot = lax.rem(index, 2)
            return pltpu.make_async_copy(
                out_buf.at[slot], columns(out_hbm, index), out_sem.at[slot]
            )

        frozen_copy(0).start()

        def spread_block(index, carry):
            local = token_ref[index] - task * rows
            spread_ids = jnp.transpose(jnp.broadcast_to(local, (128, block)))
            chosen = spread_ids == lax.broadcasted_iota(jnp.int32, (block, 128), 1)
            coef = jnp.transpose(coef_all[index].astype(F32))
            place = pl.ds(pl.multiple_of(index * block, block), block)
            for r in range(RANK):
                piece = jnp.where(chosen, coef[:, r : r + 1], 0.0).astype(BF16)
                spread[place, r * rows : (r + 1) * rows] = piece[:, :rows]
            return carry

        lax.fori_loop(0, width_count, spread_block, 0)
        if not aligned:
            wait_wide_all(exit_tasks)

        def update_chunk(index, carry):
            slot = lax.rem(index, 2)

            @pl.when(index + 1 < count)
            def _():
                frozen_copy(index + 1).start()

            if aligned:
                wait_columns(exit_tasks, index)
            exit_copy = pltpu.make_async_copy(
                factor_columns(RANK, index), exit_buf, load_sem.at[1]
            )
            exit_copy.start()
            frozen_copy(index).wait()

            @pl.when(index >= 2)
            def _():
                out_copy(index - 2).wait()

            exit_copy.wait()

            def token_block(row_block, inner_carry):
                place = pl.ds(pl.multiple_of(row_block * block, block), block)
                change = jnp.dot(
                    spread[place, :],
                    exit_buf[...].reshape(RANK * rows, chunk),
                    preferred_element_type=F32,
                )
                out_buf[slot, place, :] = (
                    frozen_buf[slot, place, :].astype(F32) + change * (1.0 / math.sqrt(RANK))
                ).astype(BF16)
                return inner_carry

            lax.fori_loop(0, width_count, token_block, 0)
            out_copy(index).start()
            return carry

        lax.fori_loop(0, count, update_chunk, 0)
        for index in range(max(0, count - 2), count):
            out_copy(index).wait()

    tok_count = width_count * block
    pl.run_scoped(
        update,
        pltpu.VMEM((tok_count, RANK * rows), BF16),
        pltpu.VMEM((RANK, rows, chunk), BF16),
        pltpu.VMEM((2, tok_count, chunk), BF16),
        pltpu.VMEM((2, tok_count, chunk), BF16),
    )

    for d in range(1, width_count):
        peer = lax.rem(wide + d, width_count)
        part_copy(peer, peer).wait_send()
        coef_copy(peer, wide).wait_send()

    def drain(step, carry):
        for d in range(1, task_count):
            hop_copy(lax.rem(task + d, task_count), task, step).wait_send()
        wait_sent(exit_tasks, step)
        return carry

    lax.fori_loop(0, steps, drain, 0)


def on_device(
    task_ids,
    embed_table,
    trunk_weight,
    trunk_bias,
    head_weight,
    head_bias,
    token_row,
    inputs,
    frozen,
):
    task_count = lax.axis_size("task")
    width_count = lax.axis_size("width")
    rows = task_ids.shape[0]
    hid = trunk_weight.shape[1]
    inner = head_weight.shape[1] // width_count
    tok_count, slice_width = inputs.shape
    step_cols = 128
    steps = inner // step_cols
    cols = step_cols * width_count
    block = tok_count // width_count
    dims = (task_count, width_count, rows, inner, slice_width, step_cols, steps, block)
    token_blocks = token_row.reshape(width_count, 1, block)
    vmem = pl.BlockSpec(memory_space=pltpu.VMEM)
    hbm = pl.BlockSpec(memory_space=pl.ANY)
    dma = pltpu.SemaphoreType.DMA
    out, _ = pl.pallas_call(
        functools.partial(exchange_kernel, dims),
        out_shape=(
            jax.ShapeDtypeStruct((tok_count, slice_width), BF16),
            jax.ShapeDtypeStruct((2 * RANK, rows, slice_width), BF16),
        ),
        in_specs=[vmem, hbm, hbm, vmem, hbm, vmem, vmem, hbm, hbm],
        out_specs=(hbm, hbm),
        scratch_shapes=[
            pltpu.VMEM((task_count, 8, rows), jnp.int32),
            pltpu.VMEM((steps, task_count, width_count, rows, step_cols), BF16),
            pltpu.VMEM((task_count, steps, width_count, rows, step_cols), BF16),
            pltpu.VMEM((width_count, RANK, block), F32),
            pltpu.VMEM((width_count, RANK, block), F32),
            pltpu.VMEM((width_count, RANK, block), BF16),
            dma((task_count,)),
            dma((task_count,)),
            dma((task_count, steps)),
            dma((task_count, steps)),
            dma((task_count, steps)),
            dma((task_count, steps)),
            dma((width_count,)),
            dma((width_count,)),
            dma((width_count,)),
            dma((width_count,)),
            dma((2,)),
            dma((2,)),
            dma((2,)),
            dma((2,)),
            dma((2,)),
        ],
        compiler_params=pltpu.CompilerParams(
            collective_id=0, has_side_effects=True, vmem_limit_bytes=58 * 1024 * 1024
        ),
        name="adapt_rows",
    )(
        task_ids.reshape(1, rows),
        embed_table,
        trunk_weight,
        trunk_bias.reshape(1, hid),
        head_weight,
        head_bias.reshape(steps, 1, cols),
        token_blocks,
        inputs,
        frozen,
    )
    return out


def solution(mesh):
    return jax.shard_map(
        on_device,
        mesh=mesh,
        in_specs=(
            P("task"),
            P(),
            P(),
            P(),
            P(None, ("task", "width")),
            P(("task", "width")),
            P("task"),
            P("task", "width"),
            P("task", "width"),
        ),
        out_specs=P("task", "width"),
        check_vma=False,
    )
```

```python
import functools
import math

import jax
import jax.numpy as jnp
from jax import lax
from jax.experimental import pallas as pl
from jax.experimental.pallas import tpu as pltpu
from jax.sharding import PartitionSpec as P

WIDTH = 8192
RANK = 16
MESH = pl.DeviceIdType.MESH
F32 = jnp.float32
BF16 = jnp.bfloat16


def exchange_kernel(
    dims,
    ids_ref,
    table_hbm,
    trunk_hbm,
    trunk_bias_ref,
    head_hbm,
    head_bias_ref,
    token_ref,
    inputs_hbm,
    spread_hbm,
    factors,
    ids_all,
    outgoing,
    stage,
    part,
    gathered,
    coef_all,
    ids_send,
    ids_recv,
    hop_send,
    hop_recv,
    wide_send,
    wide_recv,
    part_send,
    part_recv,
    coef_send,
    coef_recv,
    load_sem,
    weight_sem,
    token_sem,
    spread_sem,
):
    task_count, width_count, rows, inner, slice_width, step_cols, steps, block = dims
    cols = step_cols * width_count
    task = lax.axis_index("task")
    wide = lax.axis_index("width")
    entry_tasks = [t for t in range(task_count) if t * width_count * inner < RANK * slice_width]
    exit_tasks = [t for t in range(task_count) if t not in entry_tasks]

    hid = trunk_hbm.shape[1]
    all_rows = task_count * rows

    def target(source_task, source_wide, step):
        place = (source_task * width_count + source_wide) * inner + step * step_cols
        return factors.at[
            place // slice_width,
            :,
            pl.ds(pl.multiple_of(lax.rem(place, slice_width), step_cols), step_cols),
        ]

    def hop_copy(peer, source_task, step):
        return pltpu.make_async_remote_copy(
            src_ref=outgoing.at[step, peer],
            dst_ref=stage.at[source_task, step],
            send_sem=hop_send.at[peer, step],
            recv_sem=hop_recv.at[source_task, step],
            device_id=(peer, wide),
            device_id_type=MESH,
        )

    def send_wide(blocks, source_task, step):
        for d in range(1, width_count):
            peer = lax.rem(wide + d, width_count)
            pltpu.make_async_remote_copy(
                src_ref=blocks.at[peer],
                dst_ref=target(source_task, wide, step),
                send_sem=wide_send.at[source_task, step],
                recv_sem=wide_recv.at[source_task, step],
                device_id=(task, peer),
                device_id_type=MESH,
            ).start()
        pltpu.make_async_copy(
            blocks.at[wide], target(source_task, wide, step), wide_recv.at[source_task, step]
        ).start()

    def forward(sources, step):
        for t in sources:

            @pl.when(task != t)
            def _():
                hop_copy(t, t, step).wait_recv()
                send_wide(stage.at[t, step], t, step)

    def wait_sent(sources, step):
        for t in sources:
            sent = stage.at[t, step, pl.ds(0, width_count - 1)]
            pltpu.make_async_copy(sent, sent, wide_send.at[t, step]).wait()

    def forward_entry(step, carry):
        forward(entry_tasks, step)
        return carry

    def forward_exit(step, carry):
        wait_sent(entry_tasks, step)
        forward(exit_tasks, step)
        return carry

    def wait_wide(sources, step):
        for t in sources:
            whole = stage.at[t, step]
            pltpu.make_async_copy(whole, whole, wide_recv.at[t, step]).wait()

    def wait_wide_all(sources):
        def body(step, carry):
            wait_wide(sources, step)
            return carry

        lax.fori_loop(0, steps, body, 0)

    def generate(table, trunk, one_hot, hidden, weight, perm, flat):
        def weight_copy(step):
            return pltpu.make_async_copy(
                head_hbm.at[:, pl.ds(pl.multiple_of(step * cols, cols), cols)],
                weight.at[lax.rem(step, weight.shape[0])],
                weight_sem.at[lax.rem(step, weight.shape[0])],
            )

        table_copy = pltpu.make_async_copy(table_hbm, table, load_sem.at[0])
        trunk_copy = pltpu.make_async_copy(trunk_hbm, trunk, load_sem.at[1])
        table_copy.start()
        trunk_copy.start()
        weight_copy(0).start()

        barrier = pltpu.get_barrier_semaphore()
        for d in range(1, task_count):
            pl.semaphore_signal(
                barrier,
                inc=1,
                device_id=(lax.rem(task + d, task_count), wide),
                device_id_type=MESH,
            )
        for d in range(1, width_count):
            pl.semaphore_signal(
                barrier,
                inc=1,
                device_id=(task, lax.rem(wide + d, width_count)),
                device_id_type=MESH,
            )

        ids_all[task] = jnp.broadcast_to(ids_ref[...], (8, rows))
        place = lax.broadcasted_iota(jnp.int32, (1, cols), 1)
        source = (place % step_cols) * width_count + place // step_cols
        for top in range(0, cols, 256):
            down = lax.broadcasted_iota(jnp.int32, (256, cols), 0) + top
            perm[top : top + 256, :] = jnp.where(down == source, 1.0, 0.0).astype(BF16)

        pl.semaphore_wait(barrier, task_count + width_count - 2)

        def ids_copy(peer, slot):
            return pltpu.make_async_remote_copy(
                src_ref=ids_all.at[slot],
                dst_ref=ids_all.at[slot],
                send_sem=ids_send.at[peer],
                recv_sem=ids_recv.at[slot],
                device_id=(peer, wide),
                device_id_type=MESH,
            )

        for d in range(1, task_count):
            ids_copy(lax.rem(task + d, task_count), task).start()
        for d in range(1, task_count):
            ids_copy(lax.rem(task + d, task_count), lax.rem(task + d, task_count)).wait_recv()
        for d in range(1, task_count):
            ids_copy(lax.rem(task + d, task_count), task).wait_send()

        table_len = table.shape[0]
        for t in range(task_count):
            spread_ids = jnp.transpose(jnp.broadcast_to(ids_all[t, 0:1, :], (128, rows)))
            lane = lax.broadcasted_iota(jnp.int32, (rows, 128), 1)
            for k in range(0, table_len, 128):
                one_hot[t * rows : (t + 1) * rows, k : k + 128] = jnp.where(
                    spread_ids == lane + k, 1.0, 0.0
                ).astype(BF16)
        table_copy.wait()
        embedded = jnp.dot(one_hot[...], table[...], preferred_element_type=F32).astype(BF16)
        trunk_copy.wait()
        tile = 512
        for k in range(0, trunk.shape[1], tile):
            pre = (
                jnp.dot(embedded, trunk[:, k : k + tile], preferred_element_type=F32)
                + trunk_bias_ref[:, k : k + tile]
            )
            hidden[:, k : k + tile] = (pre / (1.0 + jnp.exp(-pre))).astype(BF16)

        def head_step(step, carry):
            weight_copy(step).wait()

            @pl.when(step + 1 < steps)
            def _():
                weight_copy(step + 1).start()

            slot = lax.rem(step, weight.shape[0])
            for k in range(0, cols, 256):
                total = jnp.dot(
                    hidden[...], weight[slot, :, k : k + 256], preferred_element_type=F32
                )
                flat[:, k : k + 256] = (total + head_bias_ref[step, :, k : k + 256]).astype(BF16)
            for k in range(0, cols, 256):
                sorted_cols = jnp.dot(
                    flat[...], perm[:, k : k + 256], preferred_element_type=F32
                ).astype(BF16)
                for s in range(0, 256, step_cols):
                    for t in range(task_count):
                        outgoing[step, t, (k + s) // step_cols] = sorted_cols[
                            t * rows : (t + 1) * rows, s : s + step_cols
                        ]
            for d in range(1, task_count):
                hop_copy(lax.rem(task + d, task_count), task, step).start()
            send_wide(outgoing.at[step, task], task, step)
            return carry

        lax.fori_loop(0, steps, head_step, 0)

    pl.run_scoped(
        generate,
        pltpu.VMEM(table_hbm.shape, BF16),
        pltpu.VMEM(trunk_hbm.shape, BF16),
        pltpu.VMEM((all_rows, table_hbm.shape[0]), BF16),
        pltpu.VMEM((all_rows, hid), BF16),
        pltpu.VMEM((min(2, steps), hid, cols), BF16),
        pltpu.VMEM((cols, cols), BF16),
        pltpu.VMEM((all_rows, cols), BF16),
    )
    lax.fori_loop(0, steps, forward_entry, 0)
    lax.fori_loop(0, steps, forward_exit, 0)

    chunk = min(256, slice_width)
    aligned = inner % slice_width == 0 and chunk % step_cols == 0
    count = slice_width // chunk

    def columns(array, index):
        return array.at[:, pl.ds(pl.multiple_of(index * chunk, chunk), chunk)]

    def factor_columns(first, index):
        return factors.at[
            pl.ds(first, RANK), :, pl.ds(pl.multiple_of(index * chunk, chunk), chunk)
        ]

    def wait_columns(sources, index):
        per = chunk // step_cols
        for turn in range(inner // slice_width):
            for q in range(per):
                wait_wide(sources, turn * (slice_width // step_cols) + index * per + q)

    def part_copy(peer, slot):
        return pltpu.make_async_remote_copy(
            src_ref=part.at[peer],
            dst_ref=gathered.at[slot],
            send_sem=part_send.at[peer],
            recv_sem=part_recv.at[slot],
            device_id=(task, peer),
            device_id_type=MESH,
        )

    def rank(entry, tokens):
        def token_copy(index):
            slot = lax.rem(index, 2)
            return pltpu.make_async_copy(
                columns(inputs_hbm, index), tokens.at[slot], token_sem.at[slot]
            )

        token_copy(0).start()
        part[...] = jnp.zeros_like(part)
        if not aligned:
            wait_wide_all(entry_tasks)

        def score_piece(index, carry):
            slot = lax.rem(index, 2)

            @pl.when(index + 1 < count)
            def _():
                token_copy(index + 1).start()

            if aligned:
                wait_columns(entry_tasks, index)
            entry_copy = pltpu.make_async_copy(factor_columns(0, index), entry, load_sem.at[0])
            entry_copy.start()
            token_copy(index).wait()
            entry_copy.wait()

            def score_block(row_block, inner_carry):
                local = token_ref[row_block] - task * rows
                chosen = lax.broadcasted_iota(jnp.int32, (rows, block), 0) == local
                place = pl.ds(pl.multiple_of(row_block * block, block), block)
                block_in = tokens[slot, place, :]
                half = RANK // 2
                for top in range(0, RANK, half):
                    scores = lax.dot_general(
                        entry[top : top + half].reshape(half * rows, chunk),
                        block_in,
                        (((1,), (1,)), ((), ())),
                        preferred_element_type=F32,
                    ).reshape(half, rows, block)
                    part[row_block, top : top + half] += jnp.sum(
                        jnp.where(chosen[None], scores, 0.0), axis=1
                    )

                @pl.when(jnp.logical_and(index == count - 1, row_block != wide))
                def _():
                    part_copy(row_block, wide).start()

                return inner_carry

            lax.fori_loop(0, width_count, score_block, 0)
            return carry

        lax.fori_loop(0, count, score_piece, 0)

    pl.run_scoped(
        rank,
        pltpu.VMEM((RANK, rows, chunk), BF16),
        pltpu.VMEM((2, width_count * block, chunk), BF16),
    )
    total = part[wide]
    for d in range(1, width_count):
        peer = lax.rem(wide + d, width_count)
        part_copy(peer, peer).wait_recv()
        total = total + gathered[peer]
    coef_all[wide] = (total * (1.0 / math.sqrt(WIDTH))).astype(BF16)

    def coef_copy(peer, slot):
        return pltpu.make_async_remote_copy(
            src_ref=coef_all.at[slot],
            dst_ref=coef_all.at[slot],
            send_sem=coef_send.at[peer],
            recv_sem=coef_recv.at[slot],
            device_id=(task, peer),
            device_id_type=MESH,
        )

    for d in range(1, width_count):
        coef_copy(lax.rem(wide + d, width_count), wide).start()
    for d in range(1, width_count):
        peer = lax.rem(wide + d, width_count)
        coef_copy(peer, peer).wait_recv()
    def spread_out(buffer):
        def spread_copy(index):
            slot = lax.rem(index, 2)
            return pltpu.make_async_copy(
                buffer.at[slot],
                spread_hbm.at[pl.ds(pl.multiple_of(index * block, block), block)],
                spread_sem.at[slot],
            )

        def spread_block(index, carry):
            @pl.when(index >= 2)
            def _():
                spread_copy(index - 2).wait()

            local = token_ref[index] - task * rows
            spread_ids = jnp.transpose(jnp.broadcast_to(local, (128, block)))
            chosen = spread_ids == lax.broadcasted_iota(jnp.int32, (block, 128), 1)
            coef = jnp.transpose(coef_all[index].astype(F32))
            for r in range(RANK):
                piece = jnp.where(chosen, coef[:, r : r + 1], 0.0).astype(BF16)
                buffer[lax.rem(index, 2), :, r * rows : (r + 1) * rows] = piece[:, :rows]
            spread_copy(index).start()
            return carry

        lax.fori_loop(0, width_count, spread_block, 0)
        for index in range(max(0, width_count - 2), width_count):
            spread_copy(index).wait()

    pl.run_scoped(spread_out, pltpu.VMEM((2, block, RANK * rows), BF16))

    for d in range(1, width_count):
        peer = lax.rem(wide + d, width_count)
        part_copy(peer, peer).wait_send()
        coef_copy(peer, wide).wait_send()

    def drain(step, carry):
        for d in range(1, task_count):
            hop_copy(lax.rem(task + d, task_count), task, step).wait_send()
        wait_sent(exit_tasks, step)
        return carry

    lax.fori_loop(0, steps, drain, 0)
    wait_wide_all(exit_tasks)


def update_kernel(spread_ref, exit_ref, frozen_ref, out_ref):
    slice_width = exit_ref.shape[2]
    exit_flat = exit_ref[...].reshape(spread_ref.shape[1], slice_width)
    tile = min(512, slice_width)
    for k in range(0, slice_width, tile):
        update = jnp.dot(
            spread_ref[...], exit_flat[:, k : k + tile], preferred_element_type=F32
        )
        out_ref[:, k : k + tile] = (
            frozen_ref[:, k : k + tile].astype(F32) + update * (1.0 / math.sqrt(RANK))
        ).astype(BF16)


def on_device(
    task_ids,
    embed_table,
    trunk_weight,
    trunk_bias,
    head_weight,
    head_bias,
    token_row,
    inputs,
    frozen,
):
    task_count = lax.axis_size("task")
    width_count = lax.axis_size("width")
    rows = task_ids.shape[0]
    hid = trunk_weight.shape[1]
    inner = head_weight.shape[1] // width_count
    tok_count, slice_width = inputs.shape
    step_cols = 128
    steps = inner // step_cols
    cols = step_cols * width_count
    block = tok_count // width_count
    dims = (task_count, width_count, rows, inner, slice_width, step_cols, steps, block)
    token_blocks = token_row.reshape(width_count, 1, block)
    vmem = pl.BlockSpec(memory_space=pltpu.VMEM)
    hbm = pl.BlockSpec(memory_space=pl.ANY)
    dma = pltpu.SemaphoreType.DMA
    spread, factors = pl.pallas_call(
        functools.partial(exchange_kernel, dims),
        out_shape=(
            jax.ShapeDtypeStruct((tok_count, RANK * rows), BF16),
            jax.ShapeDtypeStruct((2 * RANK, rows, slice_width), BF16),
        ),
        in_specs=[vmem, hbm, hbm, vmem, hbm, vmem, vmem, hbm],
        out_specs=(hbm, hbm),
        scratch_shapes=[
            pltpu.VMEM((task_count, 8, rows), jnp.int32),
            pltpu.VMEM((steps, task_count, width_count, rows, step_cols), BF16),
            pltpu.VMEM((task_count, steps, width_count, rows, step_cols), BF16),
            pltpu.VMEM((width_count, RANK, block), F32),
            pltpu.VMEM((width_count, RANK, block), F32),
            pltpu.VMEM((width_count, RANK, block), BF16),
            dma((task_count,)),
            dma((task_count,)),
            dma((task_count, steps)),
            dma((task_count, steps)),
            dma((task_count, steps)),
            dma((task_count, steps)),
            dma((width_count,)),
            dma((width_count,)),
            dma((width_count,)),
            dma((width_count,)),
            dma((2,)),
            dma((2,)),
            dma((2,)),
            dma((2,)),
        ],
        compiler_params=pltpu.CompilerParams(
            collective_id=0, has_side_effects=True, vmem_limit_bytes=58 * 1024 * 1024
        ),
        name="adapt_rows",
    )(
        task_ids.reshape(1, rows),
        embed_table,
        trunk_weight,
        trunk_bias.reshape(1, hid),
        head_weight,
        head_bias.reshape(steps, 1, cols),
        token_blocks,
        inputs,
    )
    return pl.pallas_call(
        update_kernel,
        grid=(width_count,),
        out_shape=jax.ShapeDtypeStruct((tok_count, slice_width), BF16),
        in_specs=[
            pl.BlockSpec((block, RANK * rows), lambda i: (i, 0)),
            pl.BlockSpec((RANK, rows, slice_width), lambda i: (1, 0, 0)),
            pl.BlockSpec((block, slice_width), lambda i: (i, 0)),
        ],
        out_specs=pl.BlockSpec((block, slice_width), lambda i: (i, 0)),
        compiler_params=pltpu.CompilerParams(vmem_limit_bytes=48 * 1024 * 1024),
        name="apply_update",
    )(spread, factors, frozen)


def solution(mesh):
    return jax.shard_map(
        on_device,
        mesh=mesh,
        in_specs=(
            P("task"),
            P(),
            P(),
            P(),
            P(None, ("task", "width")),
            P(("task", "width")),
            P("task"),
            P("task", "width"),
            P("task", "width"),
        ),
        out_specs=P("task", "width"),
        check_vma=False,
    )
```
